32 devices in a mesh: row: 2 (over y), col: 16 (over z, x, core).
Axes of the slice: x: 2, y: 2, z: 4, core: 2. Of those that a mesh axis runs over, the one named last changes fastest.
Arguments:
- tokens: bfloat16 [32, 1024, 1152], P(('row', 'col')), may hold values from -6 to 6
- lengths: int32 [32, 3], P(('row', 'col')), may hold values from 128 to 512, as said below
- condition: bfloat16 [32, 3, 1152], P(('row', 'col')), may hold values from -6 to 6
- keep_mask: int32 [32, 1024], P(('row', 'col')), may hold values 0 or 1
- group_mask: int32 [32, 3, 16], P(('row', 'col')), may hold values 0 or 1
- qkv_weight: bfloat16 [1152, 3456], P(('row', 'col')), may hold values from -0.1875 to 0.1875
- out_weight: bfloat16 [1152, 1152], P(('row', 'col')), may hold values from -1 to 1
- mod_weight: bfloat16 [1152, 6912], P(('row', 'col')), may hold values from -0.1875 to 0.1875
- out_bias: bfloat16 [1152], P(('row', 'col')), may hold values from -3 to 3
- mod_bias: bfloat16 [6912], P(('row', 'col')), may hold values from -2 to 2
- up_weight: bfloat16 [1152, 4608], P('row', 'col'), may hold values from -0.1875 to 0.1875
- up_bias: bfloat16 [4608], P(('row', 'col')), may hold values from -3 to 3
- down_weight: bfloat16 [4608, 1152], P('col', 'row'), may hold values from -0.1875 to 0.1875
- down_bias: bfloat16 [1152], P(('row', 'col')), may hold values from -3 to 3
- cotangent: bfloat16 [32, 1024, 1152], P(('row', 'col')), may hold values from -6 to 6
Outputs:
- block_out: bfloat16 [32, 1024, 1152], P(('row', 'col'))
- grad_tokens: float32 [32, 1024, 1152], P(('row', 'col'))
- grad_qkv: float32 [1152, 3456], P(('row', 'col'))
- grad_out: float32 [1152, 1152], P(('row', 'col'))
- grad_mod: float32 [1152, 6912], P(('row', 'col'))
- grad_outbias: float32 [1152], P(('row', 'col'))
- grad_modbias: float32 [6912], P(('row', 'col'))
- grad_up: float32 [1152, 4608], P('row', 'col')
- grad_upbias: float32 [4608], P(('row', 'col'))
- grad_down: float32 [4608, 1152], P('col', 'row')
- grad_downbias: float32 [1152], P(('row', 'col'))
The draws below stay inside these ranges and needn't reach their ends.
Inputs may be any that keep to these rules, and one draw needn't show every extreme that they name: The 3 crop lengths of a packed row sum to at most 1024; the rest of the row is padding. Some row has a crop of exactly 512 tokens and some row a crop of exactly 128.
All inputs are finite; a program needn't handle non-finite values. No bound on the sum of `keep_mask` or of `group_mask` on one device may be relied on, other than what follows from the above.
Results may differ from the reference program's by a relative error of at most 0.015.
The reference program's roundings to bfloat16 on the way count: a program that leaves them out, or rounds other values in their place, can miss the bound.
Values may be sent and summed in bfloat16 or wider, within the bound.
A program may use at most 512 MiB of HBM per device.

```python
import jax
import jax.numpy as jnp
from jax import lax

H = 16
HD = 72
FF = 4608
D = 1152
GROUPS = 16
SLOTS = 3
PACK = 1024
ROWS_ALL = 32


def draw_lengths(key, part):
    key = jax.random.fold_in(key, 17)
    first_key, second_key, third_key, pick_key = jax.random.split(key, 4)
    lowest = PACK // 8
    highest = PACK // 2
    count = ROWS_ALL
    places = jnp.arange(count, dtype=jnp.int32)
    chosen = jax.random.randint(pick_key, (), 0, count)
    first = jax.random.randint(first_key, (count,), lowest, highest + 1)
    first = jnp.where(places == chosen, highest, first)
    second_top = jnp.minimum(highest, PACK - first - lowest)
    second = jax.random.randint(second_key, (count,), lowest, second_top + 1)
    third_top = jnp.minimum(highest, PACK - first - second)
    third = jax.random.randint(third_key, (count,), lowest, third_top + 1)
    third = jnp.where(places == (chosen + 1) % count, lowest, third)
    return jnp.stack([first, second, third], axis=1).astype(jnp.int32)


def touch_ends(result, own_key, least, largest):
    shape = result.shape
    index_at = [jax.random.randint(jax.random.fold_in(own_key, axis), (), 0, shape[axis]) for axis in range(len(shape))]
    result = result.at[tuple(index_at)].set(least)
    longest = shape.index(max(shape))
    index_at[longest] = (index_at[longest] + 1) % shape[longest]
    return result.at[tuple(index_at)].set(largest)


def strengthened(entries, stream_key, source, target, parts, factor):
    owner, partner = [(jnp.arange(entries.shape[axis_at]) // (entries.shape[axis_at] // parts)).reshape([-1 if axis == axis_at else 1 for axis in range(entries.ndim)]) for axis_at in (source, target)]
    chosen = jax.random.permutation(stream_key, parts)[partner]
    strong = (owner == chosen) | (owner == (partner + parts // 2) % parts)
    return jnp.where(strong, factor * entries, entries)


def levels(key, dims, cuts, smallest, largest):
    def one(dim, shards_of):
        draws = jax.random.uniform(jax.random.fold_in(jax.random.fold_in(key, 6), dim), (shards_of,), jnp.float32, smallest / len(cuts), largest / len(cuts))
        return jnp.repeat(jnp.exp(draws), dims[dim] // shards_of).reshape((-1,) + (1,) * (len(dims) - dim - 1))

    factor_of = one(*cuts[0])
    for cut in cuts[1:]:
        factor_of = factor_of * one(*cut)
    return factor_of


def gaussian(rng, dims, deviation, bound, cuts=(), kind=jnp.bfloat16):
    result = deviation * jax.random.normal(rng, dims, jnp.float32)
    if cuts:
        result = result * levels(rng, dims, cuts, -0.22, 0.18)
    return jnp.clip(result, -bound, bound).astype(kind)


def noise_with(key, shape, spread, limit, cuts, heavy, kind=jnp.bfloat16):
    entries = spread * jax.random.normal(key, shape, jnp.float32)
    if cuts:
        entries = entries * levels(key, shape, cuts, -0.22, 0.18)
    return jnp.clip(strengthened(entries, jax.random.fold_in(key, 3), *heavy), -limit, limit).astype(kind)


def setup_inputs(seed: int = 0) -> dict:
    key_list = jax.random.split(jax.random.key(seed), 16)
    return {
        "tokens": gaussian(key_list[0], (ROWS_ALL, PACK, D), 1.0, 6.0, ((0, 32),)),
        "lengths": draw_lengths(jax.random.fold_in(key_list[15], 71), 0),
        "condition": gaussian(key_list[2], (ROWS_ALL, SLOTS, D), 1.0, 6.0, ((0, 32),)),
        "keep_mask": touch_ends((jax.random.randint(key_list[3], (ROWS_ALL, PACK), 0, 4) < 3).astype(jnp.int32), jax.random.fold_in(key_list[3], 1), 0, 1),
        "group_mask": touch_ends((jax.random.randint(key_list[4], (ROWS_ALL, SLOTS, GROUPS), 0, 4) < 3).astype(jnp.int32), jax.random.fold_in(key_list[4], 1), 0, 1),
        "qkv_weight": gaussian(key_list[5], (D, 3 * D), D ** -0.5, 0.1875, ((0, 32),)),
        "out_weight": gaussian(key_list[6], (D, D), (D // 32) ** -0.5, 1.0, ((0, 32),)),
        "mod_weight": gaussian(key_list[7], (D, 6 * D), D ** -0.5, 0.1875, ((0, 32),)),
        "out_bias": gaussian(key_list[8], (D,), 0.5, 3.0, ((0, 32),)),
        "mod_bias": gaussian(key_list[9], (6 * D,), 0.3, 2.0, ((0, 32),)),
        "up_weight": gaussian(key_list[10], (D, FF), D ** -0.5, 0.1875, ((0, 2), (1, 16))),
        "up_bias": gaussian(key_list[11], (FF,), 0.5, 3.0, ((0, 32),)),
        "down_weight": gaussian(key_list[12], (FF, D), (FF // 4) ** -0.5, 0.1875, ((0, 16), (1, 2))),
        "down_bias": gaussian(key_list[13], (D,), 0.5, 3.0, ((0, 32),)),
        "cotangent": noise_with(key_list[14], (ROWS_ALL, PACK, D), 1.0, 6.0, ((0, 32),), (0, 2, 32, 2.75)),
    }


@jax.custom_vjp
def low(v):
    return lax.optimization_barrier(v.astype(jnp.bfloat16)).astype(jnp.float32)

@jax.custom_vjp
def low_back(v):
    return v

def low_keep(v):
    return (low(v), None)

def low_pass(kept, grad):
    return (grad,)

def back_keep(v):
    return (v, None)

def back_low(kept, grad):
    return (low(grad),)
low.defvjp(low_keep, low_pass)
low_back.defvjp(back_keep, back_low)
EPS = 1e-06
CURVE = 0.7978845608028654
FLOOR = -1e+30

def gelu_tanh(value):
    return 0.5 * value * (1.0 + jnp.tanh(CURVE * (value + 0.044715 * value * value * value)))

def normalize(value):
    centred = value - lax.optimization_barrier(jnp.mean(value, axis=-1, keepdims=True))
    return centred * lax.rsqrt(lax.optimization_barrier(jnp.mean(centred * centred, axis=-1, keepdims=True)) + EPS)

def matmul(left, right):
    return jnp.dot(left, right, precision=lax.Precision.HIGHEST)

def row_forward(params, inputs, condition, lengths, keep, groups):
    qkv_weight, out_weight, mod_weight, out_bias, mod_bias, up_weight, up_bias, down_weight, down_bias = params
    width = H * HD
    ends = jnp.cumsum(lengths).astype(jnp.int32)
    places = jnp.arange(PACK, dtype=jnp.int32)
    crop = lax.optimization_barrier(jnp.sum((places[:, None] >= ends[None, :]).astype(jnp.int32), axis=1)).astype(jnp.int32)
    onehot = (crop[:, None] == jnp.arange(SLOTS, dtype=jnp.int32)[None, :]).astype(jnp.float32)
    valid = (crop < SLOTS).astype(jnp.float32)[:, None]
    cond_act = low(jax.nn.silu(condition))
    modulation = matmul(cond_act, mod_weight) + mod_bias
    per_token = matmul(onehot, modulation)
    shift_a, scale_a, gate_a, shift_m, scale_m, gate_m = jnp.split(per_token, 6, axis=1)
    attn_in = low(normalize(inputs) * (1.0 + scale_a) + shift_a)
    packed = low(low_back(matmul(attn_in, qkv_weight))).reshape(PACK, 3, H, HD)
    scores = jnp.einsum('qhd,khd->hqk', packed[:, 0], packed[:, 1], precision=lax.Precision.HIGHEST) * HD ** (-0.5)
    same = crop[:, None] == crop[None, :]
    scores = low_back(jnp.where(same[None], scores, FLOOR))
    top = lax.optimization_barrier(jnp.max(scores, axis=2, keepdims=True))
    weights = jnp.exp(scores - top)
    probs = low(weights / lax.optimization_barrier(jnp.sum(weights, axis=2, keepdims=True)))
    heads_out = jnp.einsum('hqk,khd->qhd', probs, packed[:, 2], precision=lax.Precision.HIGHEST).reshape(PACK, width)
    heads_out = low(low_back(heads_out))
    attn = low_back(matmul(heads_out, out_weight) + out_bias)
    resid = inputs + gate_a * attn
    mlp_in = low(normalize(resid) * (1.0 + scale_m) + shift_m)
    pre = low_back(matmul(mlp_in, up_weight) + up_bias)
    channel = jnp.repeat(matmul(onehot, groups), FF // GROUPS, axis=1)
    hidden = low(gelu_tanh(pre) * channel)
    mlp = low_back(matmul(hidden, down_weight) + down_bias)
    return valid * (resid + keep[:, None] * gate_m * mlp)

def reference(tokens, lengths, condition, keep_mask, group_mask, qkv_weight, out_weight, mod_weight, out_bias, mod_bias, up_weight, up_bias, down_weight, down_bias, cotangent):
    params = tuple((weight.astype(jnp.float32) for weight in (qkv_weight, out_weight, mod_weight, out_bias, mod_bias, up_weight, up_bias, down_weight, down_bias)))
    conditions = condition.astype(jnp.float32)
    keeps = keep_mask.astype(jnp.float32)
    groups = group_mask.astype(jnp.float32)

    def forward(inputs, weights):

        def step(carry, item):
            return (carry, jax.checkpoint(row_forward)(weights, *item))
        return lax.scan(step, jnp.zeros((), jnp.float32), (inputs, conditions, lengths, keeps, groups))[1]
    block_out, pullback = jax.vjp(forward, tokens.astype(jnp.float32), params)
    grad_tokens, grads = pullback(cotangent.astype(jnp.float32))
    return (block_out.astype(jnp.bfloat16), grad_tokens, grads[0], grads[1], grads[2], grads[3], grads[4], grads[5], grads[6], grads[7], grads[8])
```

```python
import functools

import jax
import jax.numpy as jnp
from jax import lax
from jax.experimental import pallas as pl
from jax.experimental.pallas import tpu as pltpu
from jax.sharding import PartitionSpec as P

H = 16
HD = 72


EPS = 1e-06
CURVE = 0.7978845608028654
FLOOR = -1e30
HEAD_BLOCK = 4
QUERY_BLOCK = 512


def gelu_tanh(value):
    return 0.5 * value * (1.0 + jnp.tanh(CURVE * (value + 0.044715 * value * value * value)))


def normalize(value):
    centred = value - jnp.mean(value, axis=-1, keepdims=True)
    inverse = lax.rsqrt(jnp.mean(centred * centred, axis=-1, keepdims=True) + EPS)
    return (centred * inverse, inverse)


def norm_back(grad, normal, inverse):
    return inverse * (
        grad
        - jnp.mean(grad, axis=-1, keepdims=True)
        - normal * jnp.mean(grad * normal, axis=-1, keepdims=True)
    )


def cross(left, right):
    return lax.dot_general(
        left, right, (((0,), (0,)), ((), ())), preferred_element_type=jnp.float32
    )


def cross_exact(left, right):
    return lax.dot_general(
        left,
        right,
        (((0,), (0,)), ((), ())),
        precision=lax.Precision.HIGHEST,
        preferred_element_type=jnp.float32,
    )


def against(left, right):
    return lax.dot_general(
        left, right, (((1,), (1,)), ((), ())), preferred_element_type=jnp.float32
    )


def scores_of(query, keys, same):
    scaled = jnp.einsum("qhd,khd->hqk", query, keys, preferred_element_type=jnp.float32) * HD ** (
        -0.5
    )
    return jnp.where(same[None], scaled, FLOOR)


def per_crop(table, crop, slots):
    total = jnp.zeros((crop.shape[0], crop.shape[1], table.shape[2]), jnp.float32)
    for slot in range(slots):
        total = total + jnp.where(crop[:, :, None] == slot, table[:, slot : slot + 1, :], 0.0)
    return total


def crop_sums(block, crop, slots):
    return jnp.stack(
        [jnp.sum(jnp.where(crop[:, :, None] == slot, block, 0.0), axis=1) for slot in range(slots)],
        axis=1,
    )


def attend_row(packed, crop):
    pack = packed.shape[0]
    parts = packed.reshape(pack, 3, H, HD)
    span = min(QUERY_BLOCK, pack)
    band = min(HEAD_BLOCK, H)
    results = []
    sums = []
    for start in range(0, pack, span):
        same = crop[start : start + span, None] == crop[None, :]
        block_results = []
        block_sums = []
        for head in range(0, H, band):
            scores = scores_of(
                parts[start : start + span, 0, head : head + band],
                parts[:, 1, head : head + band],
                same,
            )
            top = jnp.max(scores, axis=2, keepdims=True)
            weights = jnp.exp(scores - top)
            total = jnp.sum(weights, axis=2, keepdims=True)
            probs = (weights / total).astype(jnp.bfloat16)
            block_results.append(
                jnp.einsum(
                    "hqk,khd->qhd",
                    probs,
                    parts[:, 2, head : head + band],
                    preferred_element_type=jnp.float32,
                )
            )
            block_sums.append(top + jnp.log(total))
        results.append(jnp.concatenate(block_results, axis=1))
        sums.append(jnp.concatenate(block_sums, axis=0))
    heads_out = jnp.concatenate(results, axis=0).reshape(pack, H * HD).astype(jnp.bfloat16)
    return (heads_out, jnp.concatenate(sums, axis=1))


def attend_row_back(packed, crop, sums, grad_heads):
    pack = packed.shape[0]
    parts = packed.reshape(pack, 3, H, HD)
    grad_parts = grad_heads.reshape(pack, H, HD)
    span = min(QUERY_BLOCK, pack)
    band = min(HEAD_BLOCK, H)
    scale = HD ** (-0.5)
    query_grads = []
    key_grads = []
    value_grads = []
    for head in range(0, H, band):
        keys = parts[:, 1, head : head + band]
        values = parts[:, 2, head : head + band]
        key_total = jnp.zeros((pack, band, HD), jnp.float32)
        value_total = jnp.zeros((pack, band, HD), jnp.float32)
        head_query = []
        for start in range(0, pack, span):
            same = crop[start : start + span, None] == crop[None, :]
            query = parts[start : start + span, 0, head : head + band]
            grad_block = grad_parts[start : start + span, head : head + band]
            scores = scores_of(query, keys, same)
            probs = jnp.exp(scores - sums[head : head + band, start : start + span])
            value_total = value_total + jnp.einsum(
                "hqk,qhd->khd",
                probs.astype(jnp.bfloat16),
                grad_block,
                preferred_element_type=jnp.float32,
            )
            grad_probs = jnp.einsum(
                "qhd,khd->hqk", grad_block, values, preferred_element_type=jnp.float32
            )
            inner = jnp.sum(probs * grad_probs, axis=2, keepdims=True)
            grad_scores = (probs * (grad_probs - inner)).astype(jnp.bfloat16)
            head_query.append(
                jnp.einsum("hqk,khd->qhd", grad_scores, keys, preferred_element_type=jnp.float32)
                * scale
            )
            key_total = (
                key_total
                + jnp.einsum("hqk,qhd->khd", grad_scores, query, preferred_element_type=jnp.float32)
                * scale
            )
        query_grads.append(jnp.concatenate(head_query, axis=0))
        key_grads.append(key_total)
        value_grads.append(value_total)
    stacked = jnp.stack(
        [
            jnp.concatenate(query_grads, axis=1),
            jnp.concatenate(key_grads, axis=1),
            jnp.concatenate(value_grads, axis=1),
        ],
        axis=1,
    )
    return stacked.reshape(pack, 3 * H * HD).astype(jnp.bfloat16)


BOTH = ("row", "col")
MESH = pl.DeviceIdType.MESH
BF = jnp.bfloat16
F32 = jnp.float32


def place():
    col = lax.axis_index("col")
    return lax.axis_index("row"), col // 4, lax.rem(col // 2, 2), lax.rem(col, 2)


def device(y, z, x, c):
    return (y, z * 4 + x * 2 + c)


def peers():
    y, z, x, c = place()
    along = [device(y, lax.rem(z + k, 4), x, c) for k in (1, 2, 3)]
    return along + [device(1 - y, z, x, c), device(y, z, 1 - x, c), device(y, z, x, 1 - c)]


def greet():
    barrier = pltpu.get_barrier_semaphore()
    for peer in peers():
        pl.semaphore_signal(barrier, inc=1, device_id=peer, device_id_type=MESH)
    pl.semaphore_wait(barrier, 6)


class Route:
    def __init__(self, sems, base):
        self.send, self.recv = sems
        self.base = base
        y, z, x, c = place()
        self.y, self.z, self.x, self.c = y, z, x, c
        ya, xa = y + c * (1 - 2 * y), x + (1 - c) * (1 - 2 * x)
        yb, xb = y + (1 - c) * (1 - 2 * y), x + c * (1 - 2 * x)
        self.lines = [(y, x), (ya, xa), (yb, xb), (1 - y, 1 - x)]
        self.first = device(ya, z, xa, c)
        self.second = device(yb, z, xb, c)
        self.sibling = device(y, z, x, 1 - c)

    def along(self, k):
        return device(self.y, lax.rem(self.z + k, 4), self.x, self.c)

    def copy(self, i, src, dst, to):
        return pltpu.make_async_remote_copy(
            src_ref=src,
            dst_ref=dst,
            send_sem=self.send.at[self.base + i],
            recv_sem=self.recv.at[self.base + i],
            device_id=to,
            device_id_type=MESH,
        )


GATHER_SEMS = 11


class Gather(Route):
    def __init__(self, src, dst, sems, base):
        super().__init__(sems, base)
        self.src, self.dst = src, dst
        own = dst(self.y, self.z, self.x, self.c)
        self.local = pltpu.make_async_copy(src, own, self.send.at[base + 10])
        self.stage1 = [self.copy(k - 1, src, own, self.along(k)) for k in (1, 2, 3)]
        line = [dst(yy, slice(None), xx, self.c) for yy, xx in self.lines]
        self.stage2 = self.copy(3, line[0], line[0], self.first)
        self.stage3 = [self.copy(4 + w, line[w], line[w], self.second) for w in range(2)]
        self.stage4 = [self.copy(6 + w, line[w], line[w], self.sibling) for w in range(4)]

    def step(self, s):
        if s == 0:
            self.local.start()
            for copy in self.stage1:
                copy.start()
        elif s == 1:
            self.local.wait()
            for copy in self.stage1:
                copy.wait_recv()
            self.stage2.start()
            self.stage3[0].start()
            self.stage4[0].start()
        elif s == 2:
            self.stage2.wait_recv()
            self.stage3[1].start()
            self.stage4[1].start()
        elif s == 3:
            for copy in self.stage3:
                copy.wait_recv()
            self.stage4[2].start()
            self.stage4[3].start()
        elif s == 4:
            for copy in self.stage4:
                copy.wait_recv()

    def finish(self):
        for copy in self.stage1 + [self.stage2] + self.stage3 + self.stage4:
            copy.wait_send()


def gather_kernel(parts, qkv, out, mlp, all_qkv, all_out, all_mlp, send, recv):
    chunks = []

    def add(src, dst):
        chunks.append(Gather(src, dst, (send, recv), GATHER_SEMS * len(chunks)))

    greet()
    width = out.shape[1]
    for j in range(3):
        cut = pl.ds(width * j, width)
        add(qkv.at[:, cut], lambda a, b, c, d, cut=cut: all_qkv.at[a, b, c, d, :, cut])
    add(out, lambda a, b, c, d: all_out.at[a, b, c, d])
    depth = mlp.shape[0] // parts
    for j in range(parts):
        cut = pl.ds(depth * j, depth)
        add(mlp.at[cut], lambda a, b, c, d, cut=cut: all_mlp.at[a, b, c, d, cut])
    count = len(chunks)
    chunks[0].step(0)
    for t in range(count + 4):
        for s in range(5):
            if 0 <= t + 1 - s < count and not (t + 1 - s == 0 and s == 0):
                chunks[t + 1 - s].step(s)
    for chunk in chunks:
        chunk.finish()


def gather_weights(qkv, out, mlp):
    parts = 6
    sems = GATHER_SEMS * (4 + parts)
    shapes = [jax.ShapeDtypeStruct((2, 4, 2, 2) + a.shape, a.dtype) for a in (qkv, out, mlp)]
    return pl.pallas_call(
        functools.partial(gather_kernel, parts),
        out_shape=shapes,
        in_specs=[pl.BlockSpec(memory_space=pl.ANY)] * 3,
        out_specs=[pl.BlockSpec(memory_space=pl.ANY)] * 3,
        scratch_shapes=[pltpu.SemaphoreType.DMA((sems,)), pltpu.SemaphoreType.DMA((sems,))],
        compiler_params=pltpu.CompilerParams(collective_id=0, has_side_effects=True),
    )(qkv, out, mlp)


def shards(
    tokens,
    lengths,
    condition,
    keep_mask,
    group_mask,
    qkv_weight,
    out_weight,
    mod_weight,
    out_bias,
    mod_bias,
    up_weight,
    up_bias,
    down_weight,
    down_bias,
    cotangent,
):
    rows, pack, width = tokens.shape
    slots = lengths.shape[1]
    groups = group_mask.shape[2]
    count = rows * pack
    devices = lax.axis_size(BOTH)
    position = lax.axis_index(BOTH)
    side = lax.axis_index("row")
    share = width // devices
    half = up_weight.shape[0]
    silu_cond = jax.nn.silu(condition.astype(jnp.float32)).astype(jnp.bfloat16).reshape(rows * slots, width)
    small = jnp.concatenate([silu_cond.reshape(-1), out_bias, mod_bias, up_bias, down_bias])[None]
    smalls = lax.all_gather(small, BOTH, axis=0, tiled=True)
    all_cond = smalls[:, : slots * width].reshape(devices * slots, width)
    at = slots * width
    biases = []
    for part in (out_bias, mod_bias, up_bias, down_bias):
        biases.append(smalls[:, at : at + part.shape[0]].reshape(-1))
        at += part.shape[0]
    out_bias_full, mod_bias_full, up_bias_full, down_bias_full = biases
    cond_columns = lax.dynamic_slice_in_dim(all_cond, position * share, share, 1)
    mod_parts = jnp.dot(cond_columns, mod_weight, preferred_element_type=jnp.float32)
    mods = lax.psum_scatter(mod_parts, BOTH, scatter_dimension=0, tiled=True)
    up_turned = up_weight.T
    message = jnp.where(
        side == 0,
        jnp.concatenate([up_turned, down_weight], axis=1),
        jnp.concatenate([down_weight, up_turned], axis=1),
    )
    all_qkv, all_out, all_mlp = gather_weights(qkv_weight, out_weight, message)
    qkv_full = all_qkv.reshape(width, 3 * width)
    out_full = all_out.reshape(width, width)
    low, high = all_mlp.reshape(2, -1, width)
    up_full = jnp.concatenate([low[:, :half], high[:, half:]], axis=1)
    down_full = jnp.concatenate([low[:, half:], high[:, :half]], axis=1)
    hidden_units = up_full.shape[0]
    group_width = hidden_units // groups
    ends = jnp.cumsum(lengths, axis=1)
    places = jnp.arange(pack, dtype=jnp.int32)
    crop = jnp.sum((places[None, :, None] >= ends[:, None, :]).astype(jnp.int32), axis=2)
    valid = (crop < slots).astype(jnp.float32).reshape(count, 1)
    keeps = keep_mask.reshape(count, 1).astype(jnp.float32)
    mods = mods + mod_bias_full.astype(jnp.float32)
    mods = mods.reshape(rows, slots, 6 * width)
    per_token = per_crop(mods, crop, slots).reshape(count, 6 * width)
    shift_one, scale_one, gate_one, shift_two, scale_two, gate_two = jnp.split(per_token, 6, axis=1)
    channel = per_crop(group_mask.astype(jnp.float32), crop, slots).reshape(count, groups, 1)
    inputs = tokens.reshape(count, width).astype(jnp.float32)
    normal_one, inverse_one = normalize(inputs)
    first_in = (normal_one * (1.0 + scale_one) + shift_one).astype(jnp.bfloat16)
    projected = jnp.dot(first_in, qkv_full, preferred_element_type=jnp.float32).astype(jnp.bfloat16)
    packed_rows = projected.reshape(rows, pack, 3 * width)
    heads_rows, sums_rows = lax.map(lambda item: attend_row(item[0], item[1]), (packed_rows, crop))
    heads_out = heads_rows.reshape(count, width)
    attn = jnp.dot(heads_out, out_full, preferred_element_type=jnp.float32) + out_bias_full.astype(
        jnp.float32
    )
    resid = inputs + gate_one * attn
    normal_two, inverse_two = normalize(resid)
    second_in = (normal_two * (1.0 + scale_two) + shift_two).astype(jnp.bfloat16)
    pre = against(second_in, up_full) + up_bias_full.astype(
        jnp.float32
    )
    activated, gelu_pullback = jax.vjp(gelu_tanh, pre)
    hidden = (
        (activated.reshape(count, groups, group_width) * channel)
        .reshape(count, hidden_units)
        .astype(jnp.bfloat16)
    )
    mlp_out = jnp.dot(
        hidden, down_full, preferred_element_type=jnp.float32
    ) + down_bias_full.astype(jnp.float32)
    final = resid + keeps * gate_two * mlp_out
    block_out = (valid * final).astype(jnp.bfloat16).reshape(rows, pack, width)
    grad_final = valid * cotangent.reshape(count, width).astype(jnp.float32)
    grad_mlp = (keeps * gate_two * grad_final).astype(jnp.bfloat16)
    grad_gate_two = keeps * grad_final * mlp_out
    grad_down = cross(hidden, grad_mlp)
    grad_downbias = jnp.sum(grad_mlp.astype(jnp.float32), axis=0)
    grad_hidden = against(grad_mlp, down_full)
    grad_masked = (grad_hidden.reshape(count, groups, group_width) * channel).reshape(
        count, hidden_units
    )
    grad_pre = gelu_pullback(grad_masked)[0].astype(jnp.bfloat16)
    grad_up = cross(grad_pre, second_in)
    grad_upbias = jnp.sum(grad_pre.astype(jnp.float32), axis=0)
    grad_second = jnp.dot(grad_pre, up_full, preferred_element_type=jnp.float32)
    grad_resid = grad_final + norm_back(grad_second * (1.0 + scale_two), normal_two, inverse_two)
    grad_attn = (gate_one * grad_resid).astype(jnp.bfloat16)
    grad_gate_one = grad_resid * attn
    grad_out = cross(heads_out, grad_attn)
    grad_outbias = jnp.sum(grad_attn.astype(jnp.float32), axis=0)
    grad_heads = against(grad_attn, out_full).astype(jnp.bfloat16).reshape(rows, pack, width)
    low = jnp.concatenate([grad_up[:, :half], grad_down[:, :half]], axis=1)
    high = jnp.concatenate([grad_up[:, half:], grad_down[:, half:]], axis=1)
    grad_message = jnp.concatenate([low, high], axis=0).astype(jnp.bfloat16)
    grad_mine = lax.psum_scatter(grad_message, BOTH, scatter_dimension=0, tiled=True).astype(jnp.float32)
    grad_up_shard = grad_mine[:, :half].T
    grad_down_shard = grad_mine[:, half:]
    grad_projected = lax.map(
        lambda item: attend_row_back(item[0], item[1], item[2], item[3]),
        (packed_rows, crop, sums_rows, grad_heads),
    )
    grad_projected = grad_projected.reshape(count, 3 * width)
    grad_qkv = cross(first_in, grad_projected)
    grad_first = against(grad_projected, qkv_full)
    grad_tokens = grad_resid + norm_back(grad_first * (1.0 + scale_one), normal_one, inverse_one)
    grad_blocks = [
        grad_first,
        grad_first * normal_one,
        grad_gate_one,
        grad_second,
        grad_second * normal_two,
        grad_gate_two,
    ]
    grad_mods = jnp.concatenate(
        [crop_sums(block.reshape(rows, pack, width), crop, slots) for block in grad_blocks], axis=2
    )
    grad_mods = grad_mods.reshape(rows * slots, 6 * width)
    grad_qkv_shard = lax.psum_scatter(
        grad_qkv.astype(jnp.bfloat16), BOTH, scatter_dimension=0, tiled=True
    ).astype(jnp.float32)
    grad_out_shard = lax.psum_scatter(
        grad_out.astype(jnp.bfloat16), BOTH, scatter_dimension=0, tiled=True
    ).astype(jnp.float32)
    own_bias = jnp.concatenate([grad_outbias, grad_upbias, grad_downbias])[None]
    last = jnp.concatenate([grad_mods, own_bias], axis=0).astype(jnp.bfloat16)[None]
    lasts = lax.all_gather(last, BOTH, axis=0, tiled=True)
    all_grad_mods = lasts[:, :-1].reshape(-1, 6 * width)
    grad_mod_shard = cross(cond_columns, all_grad_mods)
    mod_share = 6 * width // devices
    grad_modbias_shard = jnp.sum(
        lax.dynamic_slice_in_dim(all_grad_mods, position * mod_share, mod_share, 1).astype(jnp.float32), axis=0
    )
    bias_sums = []
    at = 0
    for part in (out_bias, up_bias, down_bias):
        size = part.shape[0]
        mine = lax.dynamic_slice_in_dim(lasts[:, -1], at + position * size, size, 1)
        bias_sums.append(jnp.sum(mine.astype(jnp.float32), axis=0))
        at += size * devices
    grad_outbias_shard, grad_upbias_shard, grad_downbias_shard = bias_sums
    return (
        block_out,
        grad_tokens.reshape(rows, pack, width),
        grad_qkv_shard,
        grad_out_shard,
        grad_mod_shard,
        grad_outbias_shard,
        grad_modbias_shard,
        grad_up_shard,
        grad_upbias_shard,
        grad_down_shard,
        grad_downbias_shard,
    )


def shards_general(
    tokens,
    lengths,
    condition,
    keep_mask,
    group_mask,
    qkv_weight,
    out_weight,
    mod_weight,
    out_bias,
    mod_bias,
    up_weight,
    up_bias,
    down_weight,
    down_bias,
    cotangent,
):
    rows, pack, width = tokens.shape
    slots = lengths.shape[1]
    groups = group_mask.shape[2]
    count = rows * pack
    qkv_full, out_full, mod_full, out_bias_full, mod_bias_full, up_bias_full, down_bias_full = (
        lax.all_gather(qkv_weight, ("row", "col"), axis=0, tiled=True),
        lax.all_gather(out_weight, ("row", "col"), axis=0, tiled=True),
        lax.all_gather(mod_weight, ("row", "col"), axis=0, tiled=True),
        lax.all_gather(out_bias, ("row", "col"), axis=0, tiled=True),
        lax.all_gather(mod_bias, ("row", "col"), axis=0, tiled=True),
        lax.all_gather(up_bias, ("row", "col"), axis=0, tiled=True),
        lax.all_gather(down_bias, ("row", "col"), axis=0, tiled=True),
    )
    up_half, down_half = (
        lax.all_gather(up_weight, "col", axis=1, tiled=True),
        lax.all_gather(down_weight, "col", axis=0, tiled=True),
    )
    up_full, down_full = (
        lax.all_gather(up_half, "row", axis=0, tiled=True),
        lax.all_gather(down_half, "row", axis=1, tiled=True),
    )
    hidden_units = up_full.shape[1]
    group_width = hidden_units // groups
    ends = jnp.cumsum(lengths, axis=1)
    places = jnp.arange(pack, dtype=jnp.int32)
    crop = jnp.sum((places[None, :, None] >= ends[:, None, :]).astype(jnp.int32), axis=2)
    valid = (crop < slots).astype(jnp.float32).reshape(count, 1)
    keeps = keep_mask.reshape(count, 1).astype(jnp.float32)
    silu_cond = (
        jax.nn.silu(condition.astype(jnp.float32)).astype(jnp.bfloat16).reshape(rows * slots, width)
    )
    mods = jnp.dot(silu_cond, mod_full, preferred_element_type=jnp.float32) + mod_bias_full.astype(
        jnp.float32
    )
    mods = mods.reshape(rows, slots, 6 * width)
    per_token = per_crop(mods, crop, slots).reshape(count, 6 * width)
    shift_one, scale_one, gate_one, shift_two, scale_two, gate_two = jnp.split(per_token, 6, axis=1)
    channel = per_crop(group_mask.astype(jnp.float32), crop, slots).reshape(count, groups, 1)
    inputs = tokens.reshape(count, width).astype(jnp.float32)
    normal_one, inverse_one = normalize(inputs)
    first_in = (normal_one * (1.0 + scale_one) + shift_one).astype(jnp.bfloat16)
    projected = jnp.dot(first_in, qkv_full, preferred_element_type=jnp.float32).astype(jnp.bfloat16)
    packed_rows = projected.reshape(rows, pack, 3 * width)
    heads_rows, sums_rows = lax.map(lambda item: attend_row(item[0], item[1]), (packed_rows, crop))
    heads_out = heads_rows.reshape(count, width)
    attn = jnp.dot(heads_out, out_full, preferred_element_type=jnp.float32) + out_bias_full.astype(
        jnp.float32
    )
    resid = inputs + gate_one * attn
    normal_two, inverse_two = normalize(resid)
    second_in = (normal_two * (1.0 + scale_two) + shift_two).astype(jnp.bfloat16)
    pre = jnp.dot(second_in, up_full, preferred_element_type=jnp.float32) + up_bias_full.astype(
        jnp.float32
    )
    activated, gelu_pullback = jax.vjp(gelu_tanh, pre)
    hidden = (
        (activated.reshape(count, groups, group_width) * channel)
        .reshape(count, hidden_units)
        .astype(jnp.bfloat16)
    )
    mlp_out = jnp.dot(
        hidden, down_full, preferred_element_type=jnp.float32
    ) + down_bias_full.astype(jnp.float32)
    final = resid + keeps * gate_two * mlp_out
    block_out = (valid * final).astype(jnp.bfloat16).reshape(rows, pack, width)
    qkv_back, out_back = (
        lax.all_gather(qkv_weight, ("row", "col"), axis=0, tiled=True),
        lax.all_gather(out_weight, ("row", "col"), axis=0, tiled=True),
    )
    up_part, down_part = (
        lax.all_gather(up_weight, "col", axis=1, tiled=True),
        lax.all_gather(down_weight, "col", axis=0, tiled=True),
    )
    up_back, down_back = (
        lax.all_gather(up_part, "row", axis=0, tiled=True),
        lax.all_gather(down_part, "row", axis=1, tiled=True),
    )
    grad_final = valid * cotangent.reshape(count, width).astype(jnp.float32)
    grad_mlp = (keeps * gate_two * grad_final).astype(jnp.bfloat16)
    grad_gate_two = keeps * grad_final * mlp_out
    grad_down = cross(hidden, grad_mlp)
    grad_downbias = jnp.sum(grad_mlp.astype(jnp.float32), axis=0)
    grad_hidden = against(grad_mlp, down_back)
    grad_masked = (grad_hidden.reshape(count, groups, group_width) * channel).reshape(
        count, hidden_units
    )
    grad_pre = gelu_pullback(grad_masked)[0].astype(jnp.bfloat16)
    grad_up = cross(second_in, grad_pre)
    grad_upbias = jnp.sum(grad_pre.astype(jnp.float32), axis=0)
    grad_second = against(grad_pre, up_back)
    grad_resid = grad_final + norm_back(grad_second * (1.0 + scale_two), normal_two, inverse_two)
    grad_attn = (gate_one * grad_resid).astype(jnp.bfloat16)
    grad_gate_one = grad_resid * attn
    grad_out = cross(heads_out, grad_attn)
    grad_outbias = jnp.sum(grad_attn.astype(jnp.float32), axis=0)
    grad_heads = against(grad_attn, out_back).astype(jnp.bfloat16).reshape(rows, pack, width)
    grad_up_rows, grad_down_rows = (
        lax.psum_scatter(
            grad_up.astype(jnp.bfloat16), "row", scatter_dimension=0, tiled=True
        ).astype(jnp.float32),
        lax.psum_scatter(
            grad_down.astype(jnp.bfloat16), "row", scatter_dimension=1, tiled=True
        ).astype(jnp.float32),
    )
    grad_up_shard, grad_down_shard = (
        lax.psum_scatter(grad_up_rows, "col", scatter_dimension=1, tiled=True),
        lax.psum_scatter(grad_down_rows, "col", scatter_dimension=0, tiled=True),
    )
    grad_projected = lax.map(
        lambda item: attend_row_back(item[0], item[1], item[2], item[3]),
        (packed_rows, crop, sums_rows, grad_heads),
    )
    grad_projected = grad_projected.reshape(count, 3 * width)
    grad_qkv = cross(first_in, grad_projected)
    grad_first = against(grad_projected, qkv_back)
    grad_tokens = grad_resid + norm_back(grad_first * (1.0 + scale_one), normal_one, inverse_one)
    grad_blocks = [
        grad_first,
        grad_first * normal_one,
        grad_gate_one,
        grad_second,
        grad_second * normal_two,
        grad_gate_two,
    ]
    grad_mods = jnp.concatenate(
        [crop_sums(block.reshape(rows, pack, width), crop, slots) for block in grad_blocks], axis=2
    )
    grad_mods = grad_mods.reshape(rows * slots, 6 * width)
    cond_values = silu_cond.astype(jnp.float32)
    half_qkv, half_out, half_outbias, half_upbias, half_downbias = (
        lax.psum_scatter(
            grad_qkv.astype(jnp.bfloat16), "row", scatter_dimension=0, tiled=True
        ).astype(jnp.float32),
        lax.psum_scatter(
            grad_out.astype(jnp.bfloat16), "row", scatter_dimension=0, tiled=True
        ).astype(jnp.float32),
        lax.psum_scatter(
            grad_outbias.astype(jnp.bfloat16), "row", scatter_dimension=0, tiled=True
        ).astype(jnp.float32),
        lax.psum_scatter(
            grad_upbias.astype(jnp.bfloat16), "row", scatter_dimension=0, tiled=True
        ).astype(jnp.float32),
        lax.psum_scatter(
            grad_downbias.astype(jnp.bfloat16), "row", scatter_dimension=0, tiled=True
        ).astype(jnp.float32),
    )
    grad_qkv_shard, grad_out_shard, grad_outbias_shard, grad_upbias_shard, grad_downbias_shard = (
        lax.psum_scatter(half_qkv, "col", scatter_dimension=0, tiled=True),
        lax.psum_scatter(half_out, "col", scatter_dimension=0, tiled=True),
        lax.psum_scatter(half_outbias, "col", scatter_dimension=0, tiled=True),
        lax.psum_scatter(half_upbias, "col", scatter_dimension=0, tiled=True),
        lax.psum_scatter(half_downbias, "col", scatter_dimension=0, tiled=True),
    )
    all_cond, all_grad_mods = (
        lax.all_gather(cond_values.astype(jnp.bfloat16), ("row", "col"), axis=0, tiled=True).astype(
            cond_values.dtype
        ),
        lax.all_gather(grad_mods.astype(jnp.bfloat16), ("row", "col"), axis=0, tiled=True).astype(
            grad_mods.dtype
        ),
    )
    devices = lax.axis_size(("row", "col"))
    position = lax.axis_index(("row", "col"))
    share = width // devices
    mod_share = 6 * width // devices
    cond_columns = lax.dynamic_slice_in_dim(all_cond, position * share, share, 1)
    grad_mod_shard = cross_exact(cond_columns, all_grad_mods)
    grad_modbias_shard = jnp.sum(
        lax.dynamic_slice_in_dim(all_grad_mods, position * mod_share, mod_share, 1), axis=0
    )
    return (
        block_out,
        grad_tokens.reshape(rows, pack, width),
        grad_qkv_shard,
        grad_out_shard,
        grad_mod_shard,
        grad_outbias_shard,
        grad_modbias_shard,
        grad_up_shard,
        grad_upbias_shard,
        grad_down_shard,
        grad_downbias_shard,
    )


def solution(mesh):
    placed = (
        P(("row", "col"), None, None),
        P(("row", "col"), None),
        P(("row", "col"), None, None),
        P(("row", "col"), None),
        P(("row", "col"), None, None),
        P(("row", "col"), None),
        P(("row", "col"), None),
        P(("row", "col"), None),
        P(("row", "col")),
        P(("row", "col")),
        P("row", "col"),
        P(("row", "col")),
        P("col", "row"),
        P(("row", "col")),
        P(("row", "col"), None, None),
    )
    fitting = dict(mesh.shape) == {"row": 2, "col": 16}
    return jax.shard_map(
        shards if fitting else shards_general,
        mesh=mesh,
        in_specs=placed,
        out_specs=(
            P(("row", "col"), None, None),
            P(("row", "col"), None, None),
            P(("row", "col"), None),
            P(("row", "col"), None),
            P(("row", "col"), None),
            P(("row", "col")),
            P(("row", "col")),
            P("row", "col"),
            P(("row", "col")),
            P("col", "row"),
            P(("row", "col")),
        ),
        check_vma=False,
    )
```
